32 devices in a mesh: row: 8 (over y, x, core), col: 4 (over z).
Axes of the slice: x: 2, y: 2, z: 4, core: 2. Of those that a mesh axis runs over, the one named last changes fastest.
Arguments:
- top_inverse: float32 [8192, 8192], P('row', 'col'), may hold values from -8 to 8, as said below
- coupling: float32 [2, 8192, 4096], P(None, 'col', 'row'), may hold values from -0.0625 to 0.0625
- child_inverse: float32 [2, 4096, 1024], P(None, 'row'), may hold values from -2 to 2, as said below
- tile_mask: int32 [2, 32], P(None, 'col'), may hold values 0 or 1
Outputs:
- cross_block: float32 [1024, 2, 8192], P('col', None, 'row')
- child_block: float32 [1024, 2, 1024], P('row', None, 'col')
The draws below stay inside these ranges and needn't reach their ends.
Inputs may be any that keep to these rules, and one draw needn't show every extreme that they name: top_inverse is symmetric. `child_inverse`: each child's block is zero above its diagonal: entry (k, i, j) is 0 where i < j. `tile_mask`: the pattern applied to the coupling block per tile of 256 top-separator rows.
All inputs are finite; a program needn't handle non-finite values.
Results may differ from the reference program's by a relative error of at most 0.00011.
Values sent between devices are 32-bit elements; how exact they have to be, the bound alone decides.
No kernel may reach another device: no remote copies, remote signals or barrier semaphores. Data moves between devices by JAX's collectives and lax.ppermute only.
A program may use at most 128 MiB of HBM per device.

```python
import jax
import jax.numpy as jnp
from jax import lax

SEP = 8192
CHILD = 4096
CHILDREN = 2
PANEL = 1024
TILE = 256


def draw_top_inverse(key, part):
    key = jax.random.fold_in(key, 11)
    base = jnp.clip(jax.random.normal(key, (SEP, SEP), jnp.float32), -4.0, 4.0)
    symmetric = 0.7 * (base + base.T)
    result = symmetric + 2.0 * jnp.eye(SEP, dtype=jnp.float32)
    return jnp.clip(result, -8.0, 8.0)


def draw_child_inverse(key, part):
    key = jax.random.fold_in(key, 23)
    shape = (CHILDREN, CHILD, PANEL)
    offdiag = jnp.clip(jax.random.normal(key, shape, jnp.float32), -6.0, 6.0) / jnp.sqrt(jnp.float32(CHILD))
    diagonal = jax.random.uniform(jax.random.fold_in(key, 1), shape, jnp.float32, 0.5, 1.5)
    row_index = lax.broadcasted_iota(jnp.int32, shape, 1)
    col_index = lax.broadcasted_iota(jnp.int32, shape, 2)
    below = jnp.where(row_index > col_index, offdiag, 0.0)
    return jnp.where(row_index == col_index, diagonal, below)


def touch_ends(values, stream_key, low, top_value):
    index_at = [jax.random.randint(jax.random.fold_in(stream_key, axis), (), 0, length) for axis, length in enumerate(values.shape)]
    longest = values.shape.index(max(values.shape))
    beside = index_at[:longest] + [(index_at[longest] + 1) % values.shape[longest]] + index_at[longest + 1:]
    return values.at[tuple(index_at)].set(low).at[tuple(beside)].set(top_value)


def block_scale(rng, dims, cuts, least, top_value):
    def one(axis_at, shards_of):
        draws = jax.random.uniform(jax.random.fold_in(jax.random.fold_in(rng, 6), axis_at), (shards_of,), jnp.float32, least / len(cuts), top_value / len(cuts))
        return jnp.repeat(jnp.exp(draws), dims[axis_at] // shards_of).reshape((-1,) + (1,) * (len(dims) - axis_at - 1))

    level = one(*cuts[0])
    for cut in cuts[1:]:
        level = level * one(*cut)
    return level


def noise(stream_key, shape, scale, most, shards=(), held_as=jnp.bfloat16):
    gain = block_scale(stream_key, shape, shards, -0.22, 0.18) if shards else 1.0
    array = jax.random.normal(stream_key, shape, jnp.float32) * scale * gain
    return jnp.minimum(jnp.maximum(array, -most), most).astype(held_as)


def setup_inputs(seed: int = 0) -> dict:
    key_list = jax.random.split(jax.random.key(seed), 5)
    return {
        "top_inverse": draw_top_inverse(jax.random.fold_in(key_list[4], 71), 0),
        "coupling": noise(key_list[1], (CHILDREN, SEP, CHILD), SEP ** -0.5, 0.0625, ((1, 4), (2, 8)), jnp.float32),
        "child_inverse": draw_child_inverse(jax.random.fold_in(key_list[4], 71), 0),
        "tile_mask": touch_ends((jax.random.randint(key_list[3], (CHILDREN, SEP // TILE), 0, 4) < 3).astype(jnp.int32), jax.random.fold_in(key_list[3], 1), 0, 1),
    }


def reference(top_inverse, coupling, child_inverse, tile_mask):
    highest = lax.Precision.HIGHEST
    lower_parts = []
    diag_parts = []
    for member in range(CHILDREN):
        mask_rows = jnp.repeat(tile_mask[member].astype(jnp.float32), TILE)
        masked = coupling[member] * mask_rows[:, None]
        factor = jnp.dot(masked, child_inverse[member], precision=highest, preferred_element_type=jnp.float32)
        image = jnp.dot(top_inverse, factor, precision=highest, preferred_element_type=jnp.float32)
        gram = jnp.dot(child_inverse[member].T, child_inverse[member], precision=highest, preferred_element_type=jnp.float32)
        cross = jnp.dot(factor.T, image, precision=highest, preferred_element_type=jnp.float32)
        lower_parts.append(-image.T)
        diag_parts.append(gram + cross)
    return jnp.stack(lower_parts, axis=1), jnp.stack(diag_parts, axis=1)
```

```python
import functools

import jax
import jax.numpy as jnp
from jax import lax
from jax.experimental import pallas as pl
from jax.experimental.pallas import tpu as pltpu
from jax.sharding import PartitionSpec as P

SIZES = (4, 4)
VMEM = 48 * 2**20


def split(value):
    high = value.astype(jnp.bfloat16)
    return high, (value - high.astype(jnp.float32)).astype(jnp.bfloat16)


def dot(left, right):
    return jnp.dot(left, right, preferred_element_type=jnp.float32)


def three(left, right):
    return dot(left[0], right[0]) + (dot(left[0], right[1]) + dot(left[1], right[0]))


def after(value, event):
    return lax.optimization_barrier((value, event))[0]


def partner(size, bit):
    return [(at, at ^ bit) for at in range(size)]


def source(step, info):
    route = step // 2
    upper = info[1 + route]
    return route * 2 + jnp.where(step % 2 == 0, 1 - upper, upper)


def spans(share):
    unit = share // sum(SIZES)
    parts = [size * unit for size in SIZES]
    return [(sum(parts[:at]), part) for at, part in enumerate(parts)]


def factor_kernel(tile, chosen, cols, info, mask, own, got, left_own, left_got, *refs):
    count = len(chosen)
    outs = refs[: 4 * count]
    held = refs[4 * count :]
    step = pl.program_id(0)

    @pl.when(step == 0)
    def _():
        share = left_got.shape[2] // cols
        for at, left in enumerate((left_own.at[0], left_got.at[0])):
            for chunk, (start, part) in enumerate(chosen):
                for to in range(cols):
                    high, low = split(left[:, to * share + start : to * share + start + part])
                    into = slice(to * part, (to + 1) * part)
                    held[4 * chunk + 2 * at][:, into] = high
                    held[4 * chunk + 2 * at + 1][:, into] = low

    one, two = split(own[0]), split(got[...])
    length = got.shape[0]
    block = min(tile, length)
    first = source(step, info) * length
    for chunk in range(count):
        refs_of = held[4 * chunk : 4 * chunk + 4]
        total = three(one, (refs_of[0][...], refs_of[1][...]))
        total = total + three(two, (refs_of[2][...], refs_of[3][...]))
        for at, out in enumerate(outs[4 * chunk : 4 * chunk + 4]):

            @pl.when(step == at)
            def _(out=out, total=total):
                for start in range(0, length, block):
                    scale = mask[info[0], (first + start) // tile].astype(jnp.float32)
                    out[start : start + block, :] = total[start : start + block] * scale


def factor_call(info, mask, coupling, got, child_inverse, left_got, chosen, cols):
    length, depth = got.shape
    block = length // 4
    panel = left_got.shape[2]
    widths = [cols * span[1] for span in chosen]
    each = [width for width in widths for _ in range(4)]
    flat = pl.pallas_call(
        functools.partial(factor_kernel, length // mask.shape[1], chosen, cols),
        out_shape=[jax.ShapeDtypeStruct((block, width), jnp.float32) for width in each],
        grid_spec=pltpu.PrefetchScalarGridSpec(
            num_scalar_prefetch=2,
            grid=(4,),
            in_specs=[
                pl.BlockSpec((1, block, depth), lambda s, info, mask: (info[0], source(s, info), 0)),
                pl.BlockSpec((block, depth), lambda s, info, mask: (source(s, info), 0)),
                pl.BlockSpec((1, depth, panel), lambda s, info, mask: (info[0], 0, 0)),
                pl.BlockSpec((1, depth, panel), lambda s, info, mask: (info[0], 0, 0)),
            ],
            out_specs=[pl.BlockSpec((block, width), lambda s, info, mask: (0, 0)) for width in each],
            scratch_shapes=[pltpu.VMEM((depth, width), jnp.bfloat16) for width in each],
        ),
        compiler_params=pltpu.CompilerParams(vmem_limit_bytes=VMEM),
        cost_estimate=pl.CostEstimate(
            flops=12 * length * depth * sum(widths),
            bytes_accessed=8 * length * depth,
            transcendentals=0,
        ),
    )(info, mask, coupling, got, child_inverse, left_got)
    return [flat[4 * at : 4 * at + 4] for at in range(len(chosen))]


def image_kernel(count, info, *refs):
    parts = refs[:2]
    tops = refs[2:6]
    out, high, low = refs[6 + count :]
    half = pl.program_id(0)
    quarter = parts[0].shape[0]

    @pl.when((half == 0) & (pl.program_id(1) == 0))
    def _():
        for at, part in enumerate(parts):
            one, two = split(part[...])
            high[at * quarter : (at + 1) * quarter, :] = one
            low[at * quarter : (at + 1) * quarter, :] = two

    for core in range(2):

        @pl.when(half == core)
        def _(core=core):
            total = three(split(tops[2 * core][...]), (high[:quarter, :], low[:quarter, :]))
            total = total + three(
                split(tops[2 * core + 1][...]), (high[quarter:, :], low[quarter:, :])
            )
            part = out.shape[2]
            for to in range(out.shape[0]):
                value = total[:, to * part : (to + 1) * part]
                out[to] = value + refs[6][to] if count else value


def image_call(info, parts, tops, cols, other, before):
    length, depth = tops[0].shape
    quarter, width = parts[0].shape
    tile = min(512, length)
    tiles = length // tile
    whole = pl.BlockSpec((quarter, width), lambda h, t, info: (0, 0))
    kept = pl.BlockSpec((2 * quarter, width), lambda h, t, info: (0, 0))

    def top_map(core, route, h, t, info):
        upper = info[1 + route]
        tile_at = jnp.where(h == 0, t, tiles - 1) if core == 0 else jnp.where(h == 0, 0, t)
        return (tile_at, 2 * route + (1 - upper if other else upper))

    def out_map(h, t, info):
        return (0, jnp.where(h == 0, info[0], 1 - info[0]) * tiles + t, 0)

    result = pl.BlockSpec((cols, tile, width // cols), out_map)
    return pl.pallas_call(
        functools.partial(image_kernel, len(before)),
        out_shape=[
            jax.ShapeDtypeStruct((cols, 2 * length, width // cols), jnp.float32),
            jax.ShapeDtypeStruct((2 * quarter, width), jnp.bfloat16),
            jax.ShapeDtypeStruct((2 * quarter, width), jnp.bfloat16),
        ],
        grid_spec=pltpu.PrefetchScalarGridSpec(
            num_scalar_prefetch=1,
            grid=(2, tiles),
            in_specs=[whole] * 2
            + [
                pl.BlockSpec((tile, quarter), functools.partial(top_map, core, route))
                for core in range(2)
                for route in range(2)
            ]
            + [result] * len(before),
            out_specs=[result, kept, kept],
        ),
        compiler_params=pltpu.CompilerParams(vmem_limit_bytes=VMEM),
        cost_estimate=pl.CostEstimate(
            flops=6 * length * depth * width, bytes_accessed=4 * length * depth, transcendentals=0
        ),
    )(info, *parts, tops[0], tops[0], tops[1], tops[1], *before)


def turn_kernel(info, summed, *outs):
    value = summed[...].T
    piece = outs[0].shape[2]
    for at in range(outs[0].shape[0]):
        outs[0][at] = value[:, at * piece : (at + 1) * piece]
    length = outs[-1].shape[1]
    halves = [-value[:, :length], -value[:, length:]]
    for core in range(2):

        @pl.when(info[0] == core)
        def _(core=core):
            outs[-2][...] = halves[core]
            outs[-1][...] = halves[1 - core]


def turn_call(info, summed, cols):
    length, part = summed.shape
    vmem = pl.BlockSpec(memory_space=pltpu.VMEM)
    flat = pl.pallas_call(
        turn_kernel,
        out_shape=[jax.ShapeDtypeStruct((cols, part, length // cols), jnp.float32)]
        + [jax.ShapeDtypeStruct((part, length // 2), jnp.float32)] * 2,
        grid_spec=pltpu.PrefetchScalarGridSpec(
            num_scalar_prefetch=1, grid=(), in_specs=[vmem], out_specs=[vmem] * 3
        ),
        compiler_params=pltpu.CompilerParams(vmem_limit_bytes=VMEM),
        cost_estimate=pl.CostEstimate(
            flops=length * part, bytes_accessed=12 * length * part, transcendentals=0
        ),
    )(info, summed)
    return flat[0], flat[1:]


def cross_kernel(cols, info, image, *refs):
    held = refs[-1]
    quarters = refs[-2]
    count = (len(refs) - 2 - cols) // 4
    factors = refs[: 4 * count]
    outs = refs[4 * count : -2]
    value = jnp.concatenate([image[at] for at in range(image.shape[0])], axis=1)
    quarter = value.shape[1] // 4
    for at in range(4):
        quarters[at] = value[:, at * quarter : (at + 1) * quarter]
    lefts = []
    for other in range(2):
        places = [2 * route + (1 - info[1 + route] if other else info[1 + route]) for route in range(2)]
        lefts.append(split(jnp.concatenate([quarters[place] for place in places], axis=1)))
    for chunk, (start, part) in enumerate(spans(held.shape[2])):
        value = 0
        for other, left in enumerate(lefts):
            at = 4 * chunk + 2 * other
            value = value + three(left, (factors[at][...], factors[at + 1][...]))
        for at in range(cols):
            held[at, :, start : start + part] = value[:, at * part : (at + 1) * part]
    for shift, out in enumerate(outs):
        out[...] = held[lax.rem(info[3] + shift, cols)]


def cross_call(info, image, factors, cols):
    pieces, rows, piece = image.shape
    length = pieces * piece
    panel = sum(factor[0].shape[1] for factor in factors)
    flat = [value for factor in factors for value in factor]
    share = panel // cols
    vmem = pl.BlockSpec(memory_space=pltpu.VMEM)
    return pl.pallas_call(
        functools.partial(cross_kernel, cols),
        out_shape=[jax.ShapeDtypeStruct((rows, share), jnp.float32)] * cols,
        grid_spec=pltpu.PrefetchScalarGridSpec(
            num_scalar_prefetch=1,
            grid=(),
            in_specs=[vmem] * (1 + len(flat)),
            out_specs=[vmem] * cols,
            scratch_shapes=[
                pltpu.VMEM((4, rows, length // 4), jnp.float32),
                pltpu.VMEM((cols, rows, share), jnp.float32),
            ],
        ),
        compiler_params=pltpu.CompilerParams(vmem_limit_bytes=VMEM),
        cost_estimate=pl.CostEstimate(
            flops=6 * rows * length * panel, bytes_accessed=4 * panel * length, transcendentals=0
        ),
    )(info, image, *flat)


def solution(mesh):
    rows, cols = mesh.shape["row"], mesh.shape["col"]
    assert rows == 2 * cols
    bits = []
    while 2 ** (len(bits) + 1) < rows:
        bits.append(2 ** (len(bits) + 1))
    orders = [bits, bits[::-1]]
    pair = partner(rows, 1)
    plane = [[2 * at + core for at in range(cols)] for core in range(2)]

    def local(top_inverse, coupling, child_inverse, tile_mask):
        row = lax.axis_index("row")
        col = lax.axis_index("col")
        child = row % 2
        panel = child_inverse.shape[2]
        share = panel // cols
        uppers = [(row // order[0]) % 2 for order in orders]
        info = jnp.stack([child] + uppers + [col]).astype(jnp.int32)

        def pick(value, at):
            return lax.dynamic_index_in_dim(value, at, 0, keepdims=False)

        def ordered(kept, got, axis):
            return jnp.where(
                child == 0,
                jnp.concatenate([kept, got], axis=axis),
                jnp.concatenate([got, kept], axis=axis),
            )

        def send(values, at):
            return [
                lax.ppermute(value, "row", partner(rows, order[at]))
                for value, order in zip(values, orders)
            ]

        def halves(kept, got, at):
            keep = []
            send = []
            for one, two, order in zip(kept, got, orders):
                half = one.shape[0] // 2
                upper = (row // order[at]) % 2
                for start, into in ((upper, keep), (1 - upper, send)):
                    if isinstance(two, tuple):
                        got_part = jnp.where(start == 0, two[0], two[1])
                    else:
                        got_part = lax.dynamic_slice_in_dim(two, start * half, half, 0)
                    into.append(lax.dynamic_slice_in_dim(one, start * half, half, 0) + got_part)
            return keep, send

        def joined(mine, got, at):
            return [
                jnp.where(
                    (row // order[at]) % 2 == 0,
                    jnp.concatenate([one, two], axis=0),
                    jnp.concatenate([two, one], axis=0),
                )
                for one, two, order in zip(mine, got, orders)
            ]

        def cross_sum(total, *sent):
            for shift, block in enumerate(sent, 1):
                total = total + lax.ppermute(
                    block, "col", [(at, (at + shift) % cols) for at in range(cols)]
                )
            return total

        def gram_sum(event):
            gram = 0
            for value in after([pick(child_inverse, child), pick(chil_got, child)], event):
                gram = gram + jnp.einsum(
                    "jv,jw->vw",
                    value,
                    lax.dynamic_slice_in_dim(value, col * share, share, 1),
                    precision=lax.Precision.HIGH,
                    preferred_element_type=jnp.float32,
                )
            for bit in bits[::-1]:
                half = gram.shape[0] // 2
                upper = (row // bit) % 2
                sent = lax.dynamic_slice_in_dim(gram, (1 - upper) * half, half, 0)
                gram = lax.dynamic_slice_in_dim(gram, upper * half, half, 0)
                gram = gram + lax.ppermute(sent, "row", partner(rows, bit))
            return gram

        coup_sent = pick(coupling, 1 - child)
        chil_got = lax.ppermute(child_inverse, "row", pair)
        coup_got = lax.ppermute(coup_sent, "row", pair)
        top_got = lax.ppermute(after(top_inverse, (chil_got, coup_got)), "row", pair)

        def swapped(value):
            value = lax.all_to_all(value, "row", 0, 0, axis_index_groups=plane, tiled=True)
            value = lax.all_to_all(value, "col", 0, 0, tiled=True)
            return lax.all_to_all(value, "row", 0, 0, axis_index_groups=plane, tiled=True)

        chosen = spans(share)
        count = len(chosen)
        given = (tile_mask, coupling, coup_got, child_inverse, chil_got)
        partials = factor_call(info, *given, chosen[:1], cols)
        partials = partials + factor_call(after(info, partials), *given, chosen[1:], cols)
        factors = []
        sums = []
        gram = None
        for step in range(count + 1):
            if step < count:
                sent_one, kept_one, sent_two, kept_two = partials[step]
                kept, sent = [kept_one, kept_two], [sent_one, sent_two]
                if step == 0:
                    got = after(send(sent, 0), partials[1])
                else:
                    cuts = [jnp.split(value, 2, axis=0) for value in sent]
                    cuts = after(cuts, begun)
                    first_got = send([cut[0] for cut in cuts], 0)
                    got = list(zip(first_got, send([cut[1] for cut in cuts], 0)))
            if step:
                if step < count:
                    image = after(image, first_got)
                summed = image.reshape(-1, image.shape[2])
                summed = lax.psum_scatter(summed, "col", scatter_dimension=0, tiled=True)
                sums.append(summed)
            if step == count:
                break
            for at in range(1, len(bits)):
                kept, sent = halves(kept, got, at)
                got = send(sent, at)
            pieces = [one + two for one, two in zip(kept, got)]
            if step:
                pieces = after(pieces, image)
            if step >= 2:
                pieces = after(pieces, sums[step - 2])
            if step == 1:
                gram = gram_sum((image, sent))
            for at in reversed(range(1, len(bits))):
                pieces = joined(pieces, send(pieces, at), at)
            got = send(pieces, 0)
            image, *first = image_call(info, pieces, [top_inverse, top_got], cols, False, [])
            got = after(got, image)
            begun = got
            if step == count - 1:
                got = after(got, gram)
            image, *second = image_call(info, got, [top_inverse, top_got], cols, True, [image])
            factors.append(first + second)
        crosses = []
        outer = []
        for summed in sums:
            summed = after(summed, image)
            if crosses:
                summed = after(summed, crosses[-1])
            values, ends = turn_call(info, summed, cols)
            outer.append([ends[0], lax.ppermute(ends[1], "row", pair)])
            values = swapped(values)
            if len(outer) == count:
                kept = jnp.concatenate([ends[0] for ends in outer], axis=0)
                got = jnp.concatenate([ends[1] for ends in outer], axis=0)
                cross_block = ordered(kept[:, None], got[:, None], 1)
                values, cross_block = lax.optimization_barrier((values, cross_block))
            crosses.append(cross_call(info, values, factors, cols))
        block = jnp.concatenate([cross_sum(*cross) for cross in crosses], axis=0) + gram


        half = block.shape[0] // 2
        kept = lax.dynamic_slice_in_dim(block, child * half, half, 0)
        sent = lax.dynamic_slice_in_dim(block, (1 - child) * half, half, 0)
        got = lax.ppermute(sent, "row", pair)
        child_block = ordered(kept[:, None], got[:, None], 1)
        return cross_block, child_block

    in_specs = (P("row", "col"), P(None, "col", "row"), P(None, "row", None), P(None, "col"))
    out_specs = (P("col", None, "row"), P("row", None, "col"))
    return jax.shard_map(local, mesh=mesh, in_specs=in_specs, out_specs=out_specs, check_vma=False)
```

```python
import functools

import jax
import jax.numpy as jnp
from jax import lax
from jax.experimental import pallas as pl
from jax.experimental.pallas import tpu as pltpu
from jax.sharding import PartitionSpec as P

SIZES = (4, 4)
VMEM = 48 * 2**20


def split(value):
    high = value.astype(jnp.bfloat16)
    return high, (value - high.astype(jnp.float32)).astype(jnp.bfloat16)


def dot(left, right):
    return jnp.dot(left, right, preferred_element_type=jnp.float32)


def wide(value):
    high, low = split(value)
    return [high, low, high]


def three(left, right):
    return dot(left[0], right[0]) + (dot(left[0], right[1]) + dot(left[1], right[0]))


def after(value, event):
    return lax.optimization_barrier((value, event))[0]


def partner(size, bit):
    return [(at, at ^ bit) for at in range(size)]


def source(step, info):
    route = step // 2
    upper = info[1 + route]
    return route * 2 + jnp.where(step % 2 == 0, 1 - upper, upper)


def spans(share):
    unit = share // sum(SIZES)
    parts = [size * unit for size in SIZES]
    return [(sum(parts[:at]), part) for at, part in enumerate(parts)]


def factor_kernel(tile, chosen, cols, info, mask, own, got, left_own, left_got, *refs):
    count = len(chosen)
    outs = refs[: 4 * count]
    held = refs[4 * count :]
    step = pl.program_id(0)

    length, depth = got.shape

    @pl.when(step == 0)
    def _():
        share = left_got.shape[1] // cols
        for at, left in enumerate((left_own.at[0], left_got)):
            for chunk, (start, part) in enumerate(chosen):
                for to in range(cols):
                    high, low = split(left[:, to * share + start : to * share + start + part])
                    for row, value in enumerate((high, high, low), 3 * at):
                        rows = slice(row * depth, (row + 1) * depth)
                        held[chunk][rows, to * part : (to + 1) * part] = value

    left = jnp.concatenate(wide(own[0]) + wide(got[...]), axis=1)
    block = min(tile, length)
    first = source(step, info) * length
    for chunk in range(count):
        total = dot(left, held[chunk][...])
        for at, out in enumerate(outs[4 * chunk : 4 * chunk + 4]):

            @pl.when(step == at)
            def _(out=out, total=total):
                for start in range(0, length, block):
                    scale = mask[info[0], (first + start) // tile].astype(jnp.float32)
                    out[start : start + block, :] = total[start : start + block] * scale


def factor_call(info, mask, coupling, got, child_inverse, left_got, chosen, cols):
    length, depth = got.shape
    block = length // 4
    panel = left_got.shape[1]
    widths = [cols * span[1] for span in chosen]
    each = [width for width in widths for _ in range(4)]
    flat = pl.pallas_call(
        functools.partial(factor_kernel, length // mask.shape[1], chosen, cols),
        out_shape=[jax.ShapeDtypeStruct((block, width), jnp.float32) for width in each],
        grid_spec=pltpu.PrefetchScalarGridSpec(
            num_scalar_prefetch=2,
            grid=(4,),
            in_specs=[
                pl.BlockSpec((1, block, depth), lambda s, info, mask: (info[0], source(s, info), 0)),
                pl.BlockSpec((block, depth), lambda s, info, mask: (source(s, info), 0)),
                pl.BlockSpec((1, depth, panel), lambda s, info, mask: (info[0], 0, 0)),
                pl.BlockSpec((depth, panel), lambda s, info, mask: (0, 0)),
            ],
            out_specs=[pl.BlockSpec((block, width), lambda s, info, mask: (0, 0)) for width in each],
            scratch_shapes=[pltpu.VMEM((6 * depth, width), jnp.bfloat16) for width in widths],
        ),
        compiler_params=pltpu.CompilerParams(vmem_limit_bytes=VMEM),
        cost_estimate=pl.CostEstimate(
            flops=12 * length * depth * sum(widths),
            bytes_accessed=8 * length * depth,
            transcendentals=0,
        ),
    )(info, mask, coupling, got, child_inverse, left_got)
    return [flat[4 * at : 4 * at + 4] for at in range(len(chosen))]


def image_kernel(count, info, *refs):
    parts = refs[:2]
    tops = refs[2:6]
    out, high, low, held = refs[6 + count :]
    half = pl.program_id(0)
    quarter = parts[0].shape[0]

    @pl.when((half == 0) & (pl.program_id(1) == 0))
    def _():
        for at, part in enumerate(parts):
            one, two = split(part[...])
            high[at * quarter : (at + 1) * quarter, :] = one
            low[at * quarter : (at + 1) * quarter, :] = two
            for row, value in enumerate((one, one, two), 3 * at):
                held[row * quarter : (row + 1) * quarter, :] = value

    for core in range(2):

        @pl.when(half == core)
        def _(core=core):
            left = wide(tops[2 * core][...]) + wide(tops[2 * core + 1][...])
            total = dot(jnp.concatenate(left, axis=1), held[...])
            part = out.shape[2]
            for to in range(out.shape[0]):
                value = total[:, to * part : (to + 1) * part]
                out[to] = value + refs[6][to] if count else value


def image_call(info, parts, tops, cols, other, before):
    length, depth = tops[0].shape
    quarter, width = parts[0].shape
    tile = min(512, length)
    tiles = length // tile
    whole = pl.BlockSpec((quarter, width), lambda h, t, info: (0, 0))
    kept = pl.BlockSpec((2 * quarter, width), lambda h, t, info: (0, 0))

    def top_map(core, route, h, t, info):
        upper = info[1 + route]
        tile_at = jnp.where(h == 0, t, tiles - 1) if core == 0 else jnp.where(h == 0, 0, t)
        return (tile_at, 2 * route + (1 - upper if other else upper))

    def out_map(h, t, info):
        return (0, jnp.where(h == 0, info[0], 1 - info[0]) * tiles + t, 0)

    result = pl.BlockSpec((cols, tile, width // cols), out_map)
    return pl.pallas_call(
        functools.partial(image_kernel, len(before)),
        out_shape=[
            jax.ShapeDtypeStruct((cols, 2 * length, width // cols), jnp.float32),
            jax.ShapeDtypeStruct((2 * quarter, width), jnp.bfloat16),
            jax.ShapeDtypeStruct((2 * quarter, width), jnp.bfloat16),
        ],
        grid_spec=pltpu.PrefetchScalarGridSpec(
            num_scalar_prefetch=1,
            grid=(2, tiles),
            in_specs=[whole] * 2
            + [
                pl.BlockSpec((tile, quarter), functools.partial(top_map, core, route))
                for core in range(2)
                for route in range(2)
            ]
            + [result] * len(before),
            out_specs=[result, kept, kept],
            scratch_shapes=[pltpu.VMEM((6 * quarter, width), jnp.bfloat16)],
        ),
        compiler_params=pltpu.CompilerParams(vmem_limit_bytes=VMEM),
        cost_estimate=pl.CostEstimate(
            flops=6 * length * depth * width, bytes_accessed=4 * length * depth, transcendentals=0
        ),
    )(info, *parts, tops[0], tops[0], tops[1], tops[1], *before)


def turn_kernel(info, summed, *outs):
    value = summed[...].T
    piece = outs[0].shape[2]
    for at in range(outs[0].shape[0]):
        outs[0][at] = value[:, at * piece : (at + 1) * piece]
    length = outs[-1].shape[1]
    halves = [-value[:, :length], -value[:, length:]]
    for core in range(2):

        @pl.when(info[0] == core)
        def _(core=core):
            outs[-2][...] = halves[core]
            outs[-1][...] = halves[1 - core]


def turn_call(info, summed, cols):
    length, part = summed.shape
    vmem = pl.BlockSpec(memory_space=pltpu.VMEM)
    flat = pl.pallas_call(
        turn_kernel,
        out_shape=[jax.ShapeDtypeStruct((cols, part, length // cols), jnp.float32)]
        + [jax.ShapeDtypeStruct((part, length // 2), jnp.float32)] * 2,
        grid_spec=pltpu.PrefetchScalarGridSpec(
            num_scalar_prefetch=1, grid=(), in_specs=[vmem], out_specs=[vmem] * 3
        ),
        compiler_params=pltpu.CompilerParams(vmem_limit_bytes=VMEM),
        cost_estimate=pl.CostEstimate(
            flops=length * part, bytes_accessed=12 * length * part, transcendentals=0
        ),
    )(info, summed)
    return flat[0], flat[1:]


def cross_kernel(cols, info, image, *refs):
    held = refs[-1]
    quarters = refs[-2]
    count = (len(refs) - 2 - cols) // 4
    factors = refs[: 4 * count]
    outs = refs[4 * count : -2]
    value = jnp.concatenate([image[at] for at in range(image.shape[0])], axis=1)
    quarter = value.shape[1] // 4
    for at in range(4):
        quarters[at] = value[:, at * quarter : (at + 1) * quarter]
    lefts = []
    for other in range(2):
        places = [2 * route + (1 - info[1 + route] if other else info[1 + route]) for route in range(2)]
        lefts.append(split(jnp.concatenate([quarters[place] for place in places], axis=1)))
    for chunk, (start, part) in enumerate(spans(held.shape[2])):
        value = 0
        for other, left in enumerate(lefts):
            at = 4 * chunk + 2 * other
            value = value + three(left, (factors[at][...], factors[at + 1][...]))
        for at in range(cols):
            held[at, :, start : start + part] = value[:, at * part : (at + 1) * part]
    for shift, out in enumerate(outs):
        out[...] = held[lax.rem(info[3] + shift, cols)]


def cross_call(info, image, factors, cols):
    pieces, rows, piece = image.shape
    length = pieces * piece
    panel = sum(factor[0].shape[1] for factor in factors)
    flat = [value for factor in factors for value in factor]
    share = panel // cols
    vmem = pl.BlockSpec(memory_space=pltpu.VMEM)
    return pl.pallas_call(
        functools.partial(cross_kernel, cols),
        out_shape=[jax.ShapeDtypeStruct((rows, share), jnp.float32)] * cols,
        grid_spec=pltpu.PrefetchScalarGridSpec(
            num_scalar_prefetch=1,
            grid=(),
            in_specs=[vmem] * (1 + len(flat)),
            out_specs=[vmem] * cols,
            scratch_shapes=[
                pltpu.VMEM((4, rows, length // 4), jnp.float32),
                pltpu.VMEM((cols, rows, share), jnp.float32),
            ],
        ),
        compiler_params=pltpu.CompilerParams(vmem_limit_bytes=VMEM),
        cost_estimate=pl.CostEstimate(
            flops=6 * rows * length * panel, bytes_accessed=4 * panel * length, transcendentals=0
        ),
    )(info, image, *flat)


def solution(mesh):
    rows, cols = mesh.shape["row"], mesh.shape["col"]
    assert rows == 2 * cols
    bits = []
    while 2 ** (len(bits) + 1) < rows:
        bits.append(2 ** (len(bits) + 1))
    orders = [bits, bits[::-1]]
    pair = partner(rows, 1)
    plane = [[2 * at + core for at in range(cols)] for core in range(2)]

    def local(top_inverse, coupling, child_inverse, tile_mask):
        row = lax.axis_index("row")
        col = lax.axis_index("col")
        child = row % 2
        panel = child_inverse.shape[2]
        share = panel // cols
        uppers = [(row // order[0]) % 2 for order in orders]
        info = jnp.stack([child] + uppers + [col]).astype(jnp.int32)

        def pick(value, at):
            return lax.dynamic_index_in_dim(value, at, 0, keepdims=False)

        def ordered(kept, got, axis):
            return jnp.where(
                child == 0,
                jnp.concatenate([kept, got], axis=axis),
                jnp.concatenate([got, kept], axis=axis),
            )

        def send(values, at):
            return [
                lax.ppermute(value, "row", partner(rows, order[at]))
                for value, order in zip(values, orders)
            ]

        def halves(kept, got, at):
            keep = []
            send = []
            for one, two, order in zip(kept, got, orders):
                half = one.shape[0] // 2
                upper = (row // order[at]) % 2
                for start, into in ((upper, keep), (1 - upper, send)):
                    if isinstance(two, tuple):
                        got_part = jnp.where(start == 0, two[0], two[1])
                    else:
                        got_part = lax.dynamic_slice_in_dim(two, start * half, half, 0)
                    into.append(lax.dynamic_slice_in_dim(one, start * half, half, 0) + got_part)
            return keep, send

        def joined(mine, got, at):
            return [
                jnp.where(
                    (row // order[at]) % 2 == 0,
                    jnp.concatenate([one, two], axis=0),
                    jnp.concatenate([two, one], axis=0),
                )
                for one, two, order in zip(mine, got, orders)
            ]

        def cross_sum(total, *sent):
            for shift, block in enumerate(sent, 1):
                total = total + lax.ppermute(
                    block, "col", [(at, (at + shift) % cols) for at in range(cols)]
                )
            return total

        def gram_sum(event):
            gram = 0
            for value in after([pick(child_inverse, child), chil_got], event):
                gram = gram + jnp.einsum(
                    "jv,jw->vw",
                    value,
                    lax.dynamic_slice_in_dim(value, col * share, share, 1),
                    precision=lax.Precision.HIGH,
                    preferred_element_type=jnp.float32,
                )
            for bit in bits[::-1]:
                half = gram.shape[0] // 2
                upper = (row // bit) % 2
                sent = lax.dynamic_slice_in_dim(gram, (1 - upper) * half, half, 0)
                gram = lax.dynamic_slice_in_dim(gram, upper * half, half, 0)
                gram = gram + lax.ppermute(sent, "row", partner(rows, bit))
            return gram

        chil_sent, coup_sent = pick(child_inverse, 1 - child), pick(coupling, 1 - child)
        chil_got = lax.ppermute(chil_sent, "row", pair)
        coup_got = lax.ppermute(coup_sent, "row", pair)
        top_got = lax.ppermute(after(top_inverse, (chil_got, coup_got)), "row", pair)

        def swapped(value, event):
            value = lax.all_to_all(value, "row", 0, 0, axis_index_groups=plane, tiled=True)
            value = lax.all_to_all(value, "col", 0, 0, tiled=True)
            if event:
                value = after(value, event)
            return lax.all_to_all(value, "row", 0, 0, axis_index_groups=plane, tiled=True)

        chosen = spans(share)
        count = len(chosen)
        given = (tile_mask, coupling, coup_got, child_inverse, chil_got)
        partials = factor_call(info, *given, chosen[:1], cols)
        partials = partials + factor_call(after(info, partials), *given, chosen[1:], cols)
        factors = []
        sums = []
        gram = None
        for step in range(count + 1):
            if step < count:
                sent_one, kept_one, sent_two, kept_two = partials[step]
                kept, sent = [kept_one, kept_two], [sent_one, sent_two]
                if step == 0:
                    got = after(send(sent, 0), partials[1])
                else:
                    cuts = [jnp.split(value, 2, axis=0) for value in sent]
                    cuts = after(cuts, begun)
                    first_got = send([cut[0] for cut in cuts], 0)
                    got = list(zip(first_got, send([cut[1] for cut in cuts], 0)))
            if step:
                if step < count:
                    image = after(image, first_got)
                summed = image.reshape(-1, image.shape[2])
                summed = lax.psum_scatter(summed, "col", scatter_dimension=0, tiled=True)
                sums.append(summed)
            if step == count:
                break
            for at in range(1, len(bits)):
                kept, sent = halves(kept, got, at)
                got = send(sent, at)
            pieces = [one + two for one, two in zip(kept, got)]
            if step:
                pieces = after(pieces, image)
            if step >= 2:
                pieces = after(pieces, sums[step - 2])
            if step == 1:
                gram = gram_sum((image, sent))
            for at in reversed(range(1, len(bits))):
                pieces = joined(pieces, send(pieces, at), at)
            got = send(pieces, 0)
            image, *first = image_call(info, pieces, [top_inverse, top_got], cols, False, [])
            got = after(got, image)
            begun = got
            if step == count - 1:
                got = after(got, gram)
            image, *second = image_call(info, got, [top_inverse, top_got], cols, True, [image])
            factors.append(first + second)
        crosses = []
        outer = []
        for summed in sums:
            summed = after(summed, image)
            values, ends = turn_call(info, summed, cols)
            outer.append([ends[0], lax.ppermute(ends[1], "row", pair)])
            values = swapped(values, crosses)
            if len(outer) == count:
                kept = jnp.concatenate([ends[0] for ends in outer], axis=0)
                got = jnp.concatenate([ends[1] for ends in outer], axis=0)
                cross_block = ordered(kept[:, None], got[:, None], 1)
                values, cross_block = lax.optimization_barrier((values, cross_block))
            crosses.append(cross_call(info, values, factors, cols))
        block = jnp.concatenate([cross_sum(*cross) for cross in crosses], axis=0) + gram


        half = block.shape[0] // 2
        kept = lax.dynamic_slice_in_dim(block, child * half, half, 0)
        sent = lax.dynamic_slice_in_dim(block, (1 - child) * half, half, 0)
        got = lax.ppermute(sent, "row", pair)
        child_block = ordered(kept[:, None], got[:, None], 1)
        return cross_block, child_block

    in_specs = (P("row", "col"), P(None, "col", "row"), P(None, "row", None), P(None, "col"))
    out_specs = (P("col", None, "row"), P("row", None, "col"))
    return jax.shard_map(local, mesh=mesh, in_specs=in_specs, out_specs=out_specs, check_vma=False)
```

```python
import functools

import jax
import jax.numpy as jnp
from jax import lax
from jax.experimental import pallas as pl
from jax.experimental.pallas import tpu as pltpu
from jax.sharding import PartitionSpec as P

SIZES = (4, 4)
VMEM = 48 * 2**20


def split(value):
    high = value.astype(jnp.bfloat16)
    return high, (value - high.astype(jnp.float32)).astype(jnp.bfloat16)


def dot(left, right):
    return jnp.dot(left, right, preferred_element_type=jnp.float32)


def three(left, right):
    return dot(left[0], right[0]) + (dot(left[0], right[1]) + dot(left[1], right[0]))


def after(value, event):
    return lax.optimization_barrier((value, event))[0]


def partner(size, bit):
    return [(at, at ^ bit) for at in range(size)]


def source(step, info):
    route = step // 2
    upper = info[1 + route]
    return route * 2 + jnp.where(step % 2 == 0, 1 - upper, upper)


def spans(share):
    unit = share // sum(SIZES)
    parts = [size * unit for size in SIZES]
    return [(sum(parts[:at]), part) for at, part in enumerate(parts)]


def factor_kernel(tile, chosen, cols, info, mask, own, got, left_own, left_got, *refs):
    count = len(chosen)
    outs = refs[: 4 * count]
    held = refs[4 * count :]
    step = pl.program_id(0)

    @pl.when(step == 0)
    def _():
        share = left_got.shape[1] // cols
        for at, left in enumerate((left_own.at[0], left_got)):
            for chunk, (start, part) in enumerate(chosen):
                for to in range(cols):
                    high, low = split(left[:, to * share + start : to * share + start + part])
                    into = slice(to * part, (to + 1) * part)
                    held[4 * chunk + 2 * at][:, into] = high
                    held[4 * chunk + 2 * at + 1][:, into] = low

    one, two = split(own[0]), split(got[...])
    length = got.shape[0]
    block = min(tile, length)
    first = source(step, info) * length
    for chunk in range(count):
        refs_of = held[4 * chunk : 4 * chunk + 4]
        total = three(one, (refs_of[0][...], refs_of[1][...]))
        total = total + three(two, (refs_of[2][...], refs_of[3][...]))
        for at, out in enumerate(outs[4 * chunk : 4 * chunk + 4]):

            @pl.when(step == at)
            def _(out=out, total=total):
                for start in range(0, length, block):
                    scale = mask[info[0], (first + start) // tile].astype(jnp.float32)
                    out[start : start + block, :] = total[start : start + block] * scale


def factor_call(info, mask, coupling, got, child_inverse, left_got, chosen, cols):
    length, depth = got.shape
    block = length // 4
    panel = left_got.shape[1]
    widths = [cols * span[1] for span in chosen]
    each = [width for width in widths for _ in range(4)]
    flat = pl.pallas_call(
        functools.partial(factor_kernel, length // mask.shape[1], chosen, cols),
        out_shape=[jax.ShapeDtypeStruct((block, width), jnp.float32) for width in each],
        grid_spec=pltpu.PrefetchScalarGridSpec(
            num_scalar_prefetch=2,
            grid=(4,),
            in_specs=[
                pl.BlockSpec((1, block, depth), lambda s, info, mask: (info[0], source(s, info), 0)),
                pl.BlockSpec((block, depth), lambda s, info, mask: (source(s, info), 0)),
                pl.BlockSpec((1, depth, panel), lambda s, info, mask: (info[0], 0, 0)),
                pl.BlockSpec((depth, panel), lambda s, info, mask: (0, 0)),
            ],
            out_specs=[pl.BlockSpec((block, width), lambda s, info, mask: (0, 0)) for width in each],
            scratch_shapes=[pltpu.VMEM((depth, width), jnp.bfloat16) for width in each],
        ),
        compiler_params=pltpu.CompilerParams(vmem_limit_bytes=VMEM),
        cost_estimate=pl.CostEstimate(
            flops=12 * length * depth * sum(widths),
            bytes_accessed=8 * length * depth,
            transcendentals=0,
        ),
    )(info, mask, coupling, got, child_inverse, left_got)
    return [flat[4 * at : 4 * at + 4] for at in range(len(chosen))]


def image_kernel(count, info, *refs):
    parts = refs[:2]
    tops = refs[2:6]
    out, high, low = refs[6 + count :]
    half = pl.program_id(0)
    quarter = parts[0].shape[0]

    @pl.when((half == 0) & (pl.program_id(1) == 0))
    def _():
        for at, part in enumerate(parts):
            one, two = split(part[...])
            high[at * quarter : (at + 1) * quarter, :] = one
            low[at * quarter : (at + 1) * quarter, :] = two

    for core in range(2):

        @pl.when(half == core)
        def _(core=core):
            total = three(split(tops[2 * core][...]), (high[:quarter, :], low[:quarter, :]))
            total = total + three(
                split(tops[2 * core + 1][...]), (high[quarter:, :], low[quarter:, :])
            )
            part = out.shape[2]
            for to in range(out.shape[0]):
                value = total[:, to * part : (to + 1) * part]
                out[to] = value + refs[6][to] if count else value


def image_call(info, parts, tops, cols, other, before):
    length, depth = tops[0].shape
    quarter, width = parts[0].shape
    tile = min(512, length)
    tiles = length // tile
    whole = pl.BlockSpec((quarter, width), lambda h, t, info: (0, 0))
    kept = pl.BlockSpec((2 * quarter, width), lambda h, t, info: (0, 0))

    def top_map(core, route, h, t, info):
        upper = info[1 + route]
        tile_at = jnp.where(h == 0, t, tiles - 1) if core == 0 else jnp.where(h == 0, 0, t)
        return (tile_at, 2 * route + (1 - upper if other else upper))

    def out_map(h, t, info):
        return (0, jnp.where(h == 0, info[0], 1 - info[0]) * tiles + t, 0)

    result = pl.BlockSpec((cols, tile, width // cols), out_map)
    return pl.pallas_call(
        functools.partial(image_kernel, len(before)),
        out_shape=[
            jax.ShapeDtypeStruct((cols, 2 * length, width // cols), jnp.float32),
            jax.ShapeDtypeStruct((2 * quarter, width), jnp.bfloat16),
            jax.ShapeDtypeStruct((2 * quarter, width), jnp.bfloat16),
        ],
        grid_spec=pltpu.PrefetchScalarGridSpec(
            num_scalar_prefetch=1,
            grid=(2, tiles),
            in_specs=[whole] * 2
            + [
                pl.BlockSpec((tile, quarter), functools.partial(top_map, core, route))
                for core in range(2)
                for route in range(2)
            ]
            + [result] * len(before),
            out_specs=[result, kept, kept],
        ),
        compiler_params=pltpu.CompilerParams(vmem_limit_bytes=VMEM),
        cost_estimate=pl.CostEstimate(
            flops=6 * length * depth * width, bytes_accessed=4 * length * depth, transcendentals=0
        ),
    )(info, *parts, tops[0], tops[0], tops[1], tops[1], *before)


def turn_kernel(info, summed, *outs):
    value = summed[...].T
    piece = outs[0].shape[2]
    for at in range(outs[0].shape[0]):
        outs[0][at] = value[:, at * piece : (at + 1) * piece]
    length = outs[-1].shape[1]
    halves = [-value[:, :length], -value[:, length:]]
    for core in range(2):

        @pl.when(info[0] == core)
        def _(core=core):
            outs[-2][...] = halves[core]
            outs[-1][...] = halves[1 - core]


def turn_call(info, summed, cols):
    length, part = summed.shape
    vmem = pl.BlockSpec(memory_space=pltpu.VMEM)
    flat = pl.pallas_call(
        turn_kernel,
        out_shape=[jax.ShapeDtypeStruct((cols, part, length // cols), jnp.float32)]
        + [jax.ShapeDtypeStruct((part, length // 2), jnp.float32)] * 2,
        grid_spec=pltpu.PrefetchScalarGridSpec(
            num_scalar_prefetch=1, grid=(), in_specs=[vmem], out_specs=[vmem] * 3
        ),
        compiler_params=pltpu.CompilerParams(vmem_limit_bytes=VMEM),
        cost_estimate=pl.CostEstimate(
            flops=length * part, bytes_accessed=12 * length * part, transcendentals=0
        ),
    )(info, summed)
    return flat[0], flat[1:]


def cross_kernel(cols, info, image, *refs):
    held = refs[-1]
    quarters = refs[-2]
    count = (len(refs) - 2 - cols) // 4
    factors = refs[: 4 * count]
    outs = refs[4 * count : -2]
    value = jnp.concatenate([image[at] for at in range(image.shape[0])], axis=1)
    quarter = value.shape[1] // 4
    for at in range(4):
        quarters[at] = value[:, at * quarter : (at + 1) * quarter]
    lefts = []
    for other in range(2):
        places = [2 * route + (1 - info[1 + route] if other else info[1 + route]) for route in range(2)]
        lefts.append(split(jnp.concatenate([quarters[place] for place in places], axis=1)))
    for chunk, (start, part) in enumerate(spans(held.shape[2])):
        value = 0
        for other, left in enumerate(lefts):
            at = 4 * chunk + 2 * other
            value = value + three(left, (factors[at][...], factors[at + 1][...]))
        for at in range(cols):
            held[at, :, start : start + part] = value[:, at * part : (at + 1) * part]
    for shift, out in enumerate(outs):
        out[...] = held[lax.rem(info[3] + shift, cols)]


def cross_call(info, image, factors, cols):
    pieces, rows, piece = image.shape
    length = pieces * piece
    panel = sum(factor[0].shape[1] for factor in factors)
    flat = [value for factor in factors for value in factor]
    share = panel // cols
    vmem = pl.BlockSpec(memory_space=pltpu.VMEM)
    return pl.pallas_call(
        functools.partial(cross_kernel, cols),
        out_shape=[jax.ShapeDtypeStruct((rows, share), jnp.float32)] * cols,
        grid_spec=pltpu.PrefetchScalarGridSpec(
            num_scalar_prefetch=1,
            grid=(),
            in_specs=[vmem] * (1 + len(flat)),
            out_specs=[vmem] * cols,
            scratch_shapes=[
                pltpu.VMEM((4, rows, length // 4), jnp.float32),
                pltpu.VMEM((cols, rows, share), jnp.float32),
            ],
        ),
        compiler_params=pltpu.CompilerParams(vmem_limit_bytes=VMEM),
        cost_estimate=pl.CostEstimate(
            flops=6 * rows * length * panel, bytes_accessed=4 * panel * length, transcendentals=0
        ),
    )(info, image, *flat)


def solution(mesh):
    rows, cols = mesh.shape["row"], mesh.shape["col"]
    assert rows == 2 * cols
    bits = []
    while 2 ** (len(bits) + 1) < rows:
        bits.append(2 ** (len(bits) + 1))
    orders = [bits, bits[::-1]]
    pair = partner(rows, 1)
    plane = [[2 * at + core for at in range(cols)] for core in range(2)]

    def local(top_inverse, coupling, child_inverse, tile_mask):
        row = lax.axis_index("row")
        col = lax.axis_index("col")
        child = row % 2
        panel = child_inverse.shape[2]
        share = panel // cols
        uppers = [(row // order[0]) % 2 for order in orders]
        info = jnp.stack([child] + uppers + [col]).astype(jnp.int32)

        def pick(value, at):
            return lax.dynamic_index_in_dim(value, at, 0, keepdims=False)

        def ordered(kept, got, axis):
            return jnp.where(
                child == 0,
                jnp.concatenate([kept, got], axis=axis),
                jnp.concatenate([got, kept], axis=axis),
            )

        def send(values, at):
            return [
                lax.ppermute(value, "row", partner(rows, order[at]))
                for value, order in zip(values, orders)
            ]

        def halves(kept, got, at):
            keep = []
            send = []
            for one, two, order in zip(kept, got, orders):
                half = one.shape[0] // 2
                upper = (row // order[at]) % 2
                for start, into in ((upper, keep), (1 - upper, send)):
                    if isinstance(two, tuple):
                        got_part = jnp.where(start == 0, two[0], two[1])
                    else:
                        got_part = lax.dynamic_slice_in_dim(two, start * half, half, 0)
                    into.append(lax.dynamic_slice_in_dim(one, start * half, half, 0) + got_part)
            return keep, send

        def joined(mine, got, at):
            return [
                jnp.where(
                    (row // order[at]) % 2 == 0,
                    jnp.concatenate([one, two], axis=0),
                    jnp.concatenate([two, one], axis=0),
                )
                for one, two, order in zip(mine, got, orders)
            ]

        def cross_sum(total, *sent):
            for shift, block in enumerate(sent, 1):
                total = total + lax.ppermute(
                    block, "col", [(at, (at + shift) % cols) for at in range(cols)]
                )
            return total

        def gram_sum(event):
            gram = 0
            for value in after([pick(child_inverse, child), chil_got], event):
                gram = gram + jnp.einsum(
                    "jv,jw->vw",
                    value,
                    lax.dynamic_slice_in_dim(value, col * share, share, 1),
                    precision=lax.Precision.HIGH,
                    preferred_element_type=jnp.float32,
                )
            for bit in bits[::-1]:
                half = gram.shape[0] // 2
                upper = (row // bit) % 2
                sent = lax.dynamic_slice_in_dim(gram, (1 - upper) * half, half, 0)
                gram = lax.dynamic_slice_in_dim(gram, upper * half, half, 0)
                gram = gram + lax.ppermute(sent, "row", partner(rows, bit))
            return gram

        chil_sent, coup_sent = pick(child_inverse, 1 - child), pick(coupling, 1 - child)
        chil_got = lax.ppermute(chil_sent, "row", pair)
        coup_got = lax.ppermute(coup_sent, "row", pair)
        top_got = lax.ppermute(after(top_inverse, (chil_got, coup_got)), "row", pair)

        def swapped(value, event):
            value = lax.all_to_all(value, "row", 0, 0, axis_index_groups=plane, tiled=True)
            value = lax.all_to_all(value, "col", 0, 0, tiled=True)
            if event:
                value = after(value, event)
            return lax.all_to_all(value, "row", 0, 0, axis_index_groups=plane, tiled=True)

        chosen = spans(share)
        count = len(chosen)
        given = (tile_mask, coupling, coup_got, child_inverse, chil_got)
        partials = factor_call(info, *given, chosen[:1], cols)
        partials = partials + factor_call(after(info, partials), *given, chosen[1:], cols)
        factors = []
        sums = []
        gram = None
        for step in range(count + 1):
            if step < count:
                sent_one, kept_one, sent_two, kept_two = partials[step]
                kept, sent = [kept_one, kept_two], [sent_one, sent_two]
                if step == 0:
                    got = after(send(sent, 0), partials[1])
                else:
                    cuts = [jnp.split(value, 2, axis=0) for value in sent]
                    cuts = after(cuts, begun)
                    first_got = send([cut[0] for cut in cuts], 0)
                    got = list(zip(first_got, send([cut[1] for cut in cuts], 0)))
            if step:
                if step < count:
                    image = after(image, first_got)
                summed = image.reshape(-1, image.shape[2])
                summed = lax.psum_scatter(summed, "col", scatter_dimension=0, tiled=True)
                sums.append(summed)
            if step == count:
                break
            for at in range(1, len(bits)):
                kept, sent = halves(kept, got, at)
                got = send(sent, at)
            pieces = [one + two for one, two in zip(kept, got)]
            if step:
                pieces = after(pieces, image)
            if step >= 2:
                pieces = after(pieces, sums[step - 2])
            if step == 1:
                gram = gram_sum((image, sent))
            for at in reversed(range(1, len(bits))):
                pieces = joined(pieces, send(pieces, at), at)
            got = send(pieces, 0)
            image, *first = image_call(info, pieces, [top_inverse, top_got], cols, False, [])
            got = after(got, image)
            begun = got
            if step == count - 1:
                got = after(got, gram)
            image, *second = image_call(info, got, [top_inverse, top_got], cols, True, [image])
            factors.append(first + second)
        crosses = []
        outer = []
        for summed in sums:
            summed = after(summed, image)
            if crosses:
                summed = after(summed, values)
            values, ends = turn_call(info, summed, cols)
            outer.append([ends[0], lax.ppermute(ends[1], "row", pair)])
            values = swapped(values, crosses)
            if len(outer) == count:
                kept = jnp.concatenate([ends[0] for ends in outer], axis=0)
                got = jnp.concatenate([ends[1] for ends in outer], axis=0)
                cross_block = ordered(kept[:, None], got[:, None], 1)
                values, cross_block = lax.optimization_barrier((values, cross_block))
            crosses.append(cross_call(info, values, factors, cols))
        block = jnp.concatenate([cross_sum(*cross) for cross in crosses], axis=0) + gram


        half = block.shape[0] // 2
        kept = lax.dynamic_slice_in_dim(block, child * half, half, 0)
        sent = lax.dynamic_slice_in_dim(block, (1 - child) * half, half, 0)
        got = lax.ppermute(sent, "row", pair)
        child_block = ordered(kept[:, None], got[:, None], 1)
        return cross_block, child_block

    in_specs = (P("row", "col"), P(None, "col", "row"), P(None, "row", None), P(None, "col"))
    out_specs = (P("col", None, "row"), P("row", None, "col"))
    return jax.shard_map(local, mesh=mesh, in_specs=in_specs, out_specs=out_specs, check_vma=False)
```

```python
import functools

import jax
import jax.numpy as jnp
from jax import lax
from jax.experimental import pallas as pl
from jax.experimental.pallas import tpu as pltpu
from jax.sharding import PartitionSpec as P

SIZES = (4, 4)
VMEM = 48 * 2**20


def split(value):
    high = value.astype(jnp.bfloat16)
    return high, (value - high.astype(jnp.float32)).astype(jnp.bfloat16)


def dot(left, right):
    return jnp.dot(left, right, preferred_element_type=jnp.float32)


def three(left, right):
    return dot(left[0], right[0]) + (dot(left[0], right[1]) + dot(left[1], right[0]))


def after(value, event):
    return lax.optimization_barrier((value, event))[0]


def partner(size, bit):
    return [(at, at ^ bit) for at in range(size)]


def source(step, info):
    route = step // 2
    upper = info[1 + route]
    return route * 2 + jnp.where(step % 2 == 0, 1 - upper, upper)


def spans(share):
    unit = share // sum(SIZES)
    parts = [size * unit for size in SIZES]
    return [(sum(parts[:at]), part) for at, part in enumerate(parts)]


def factor_kernel(tile, chosen, cols, info, mask, own, got, left_own, left_got, *refs):
    count = len(chosen)
    outs = refs[: 4 * count]
    held = refs[4 * count :]
    step = pl.program_id(0)

    @pl.when(step == 0)
    def _():
        share = left_got.shape[1] // cols
        for at, left in enumerate((left_own.at[0], left_got)):
            for chunk, (start, part) in enumerate(chosen):
                for to in range(cols):
                    high, low = split(left[:, to * share + start : to * share + start + part])
                    into = slice(to * part, (to + 1) * part)
                    held[4 * chunk + 2 * at][:, into] = high
                    held[4 * chunk + 2 * at + 1][:, into] = low

    one, two = split(own[0]), split(got[...])
    length = got.shape[0]
    block = min(tile, length)
    first = source(step, info) * length
    for chunk in range(count):
        refs_of = held[4 * chunk : 4 * chunk + 4]
        total = three(one, (refs_of[0][...], refs_of[1][...]))
        total = total + three(two, (refs_of[2][...], refs_of[3][...]))
        for at, out in enumerate(outs[4 * chunk : 4 * chunk + 4]):

            @pl.when(step == at)
            def _(out=out, total=total):
                for start in range(0, length, block):
                    scale = mask[info[0], (first + start) // tile].astype(jnp.float32)
                    out[start : start + block, :] = total[start : start + block] * scale


def factor_call(info, mask, coupling, got, child_inverse, left_got, chosen, cols):
    length, depth = got.shape
    block = length // 4
    panel = left_got.shape[1]
    widths = [cols * span[1] for span in chosen]
    each = [width for width in widths for _ in range(4)]
    flat = pl.pallas_call(
        functools.partial(factor_kernel, length // mask.shape[1], chosen, cols),
        out_shape=[jax.ShapeDtypeStruct((block, width), jnp.float32) for width in each],
        grid_spec=pltpu.PrefetchScalarGridSpec(
            num_scalar_prefetch=2,
            grid=(4,),
            in_specs=[
                pl.BlockSpec((1, block, depth), lambda s, info, mask: (info[0], source(s, info), 0)),
                pl.BlockSpec((block, depth), lambda s, info, mask: (source(s, info), 0)),
                pl.BlockSpec((1, depth, panel), lambda s, info, mask: (info[0], 0, 0)),
                pl.BlockSpec((depth, panel), lambda s, info, mask: (0, 0)),
            ],
            out_specs=[pl.BlockSpec((block, width), lambda s, info, mask: (0, 0)) for width in each],
            scratch_shapes=[pltpu.VMEM((depth, width), jnp.bfloat16) for width in each],
        ),
        compiler_params=pltpu.CompilerParams(vmem_limit_bytes=VMEM),
        cost_estimate=pl.CostEstimate(
            flops=12 * length * depth * sum(widths),
            bytes_accessed=8 * length * depth,
            transcendentals=0,
        ),
    )(info, mask, coupling, got, child_inverse, left_got)
    return [flat[4 * at : 4 * at + 4] for at in range(len(chosen))]


def image_kernel(count, info, *refs):
    parts = refs[:4]
    tops = refs[4:8]
    out, high, low = refs[8 + count :]
    half = pl.program_id(0)
    length = parts[0].shape[0]
    quarter = 2 * length

    @pl.when((half == 0) & (pl.program_id(1) == 0))
    def _():
        for at, part in enumerate(parts):
            upper = info[4 + at // 2]
            place = upper if at % 2 == 0 else 1 - upper
            rows = pl.ds(pl.multiple_of((at // 2 * 2 + place) * length, length), length)
            one, two = split(part[...])
            high[rows, :] = one
            low[rows, :] = two

    for core in range(2):

        @pl.when(half == core)
        def _(core=core):
            total = three(split(tops[2 * core][...]), (high[:quarter, :], low[:quarter, :]))
            total = total + three(
                split(tops[2 * core + 1][...]), (high[quarter:, :], low[quarter:, :])
            )
            part = out.shape[2]
            for to in range(out.shape[0]):
                value = total[:, to * part : (to + 1) * part]
                out[to] = value + refs[8][to] if count else value


def image_call(info, parts, tops, cols, other, before):
    length, depth = tops[0].shape
    eighth, width = parts[0].shape
    quarter = 2 * eighth
    tile = min(512, length)
    tiles = length // tile
    whole = pl.BlockSpec((eighth, width), lambda h, t, info: (0, 0))
    kept = pl.BlockSpec((2 * quarter, width), lambda h, t, info: (0, 0))

    def top_map(core, route, h, t, info):
        upper = info[1 + route]
        tile_at = jnp.where(h == 0, t, tiles - 1) if core == 0 else jnp.where(h == 0, 0, t)
        return (tile_at, 2 * route + (1 - upper if other else upper))

    def out_map(h, t, info):
        return (0, jnp.where(h == 0, info[0], 1 - info[0]) * tiles + t, 0)

    result = pl.BlockSpec((cols, tile, width // cols), out_map)
    return pl.pallas_call(
        functools.partial(image_kernel, len(before)),
        out_shape=[
            jax.ShapeDtypeStruct((cols, 2 * length, width // cols), jnp.float32),
            jax.ShapeDtypeStruct((2 * quarter, width), jnp.bfloat16),
            jax.ShapeDtypeStruct((2 * quarter, width), jnp.bfloat16),
        ],
        grid_spec=pltpu.PrefetchScalarGridSpec(
            num_scalar_prefetch=1,
            grid=(2, tiles),
            in_specs=[whole] * 4
            + [
                pl.BlockSpec((tile, quarter), functools.partial(top_map, core, route))
                for core in range(2)
                for route in range(2)
            ]
            + [result] * len(before),
            out_specs=[result, kept, kept],
        ),
        compiler_params=pltpu.CompilerParams(vmem_limit_bytes=VMEM),
        cost_estimate=pl.CostEstimate(
            flops=6 * length * depth * width, bytes_accessed=4 * length * depth, transcendentals=0
        ),
    )(info, *parts, tops[0], tops[0], tops[1], tops[1], *before)


def turn_kernel(info, summed, *outs):
    value = summed[...].T
    piece = outs[0].shape[2]
    for at in range(outs[0].shape[0]):
        outs[0][at] = value[:, at * piece : (at + 1) * piece]
    length = outs[-1].shape[1]
    halves = [-value[:, :length], -value[:, length:]]
    for core in range(2):

        @pl.when(info[0] == core)
        def _(core=core):
            outs[-2][...] = halves[core]
            outs[-1][...] = halves[1 - core]


def turn_call(info, summed, cols):
    length, part = summed.shape
    vmem = pl.BlockSpec(memory_space=pltpu.VMEM)
    flat = pl.pallas_call(
        turn_kernel,
        out_shape=[jax.ShapeDtypeStruct((cols, part, length // cols), jnp.float32)]
        + [jax.ShapeDtypeStruct((part, length // 2), jnp.float32)] * 2,
        grid_spec=pltpu.PrefetchScalarGridSpec(
            num_scalar_prefetch=1, grid=(), in_specs=[vmem], out_specs=[vmem] * 3
        ),
        compiler_params=pltpu.CompilerParams(vmem_limit_bytes=VMEM),
        cost_estimate=pl.CostEstimate(
            flops=length * part, bytes_accessed=12 * length * part, transcendentals=0
        ),
    )(info, summed)
    return flat[0], flat[1:]


def cross_kernel(cols, info, image, *refs):
    held = refs[-1]
    quarters = refs[-2]
    count = (len(refs) - 2 - cols) // 4
    factors = refs[: 4 * count]
    outs = refs[4 * count : -2]
    value = jnp.concatenate([image[at] for at in range(image.shape[0])], axis=1)
    quarter = value.shape[1] // 4
    for at in range(4):
        quarters[at] = value[:, at * quarter : (at + 1) * quarter]
    lefts = []
    for other in range(2):
        places = [2 * route + (1 - info[1 + route] if other else info[1 + route]) for route in range(2)]
        lefts.append(split(jnp.concatenate([quarters[place] for place in places], axis=1)))
    for chunk, (start, part) in enumerate(spans(held.shape[2])):
        value = 0
        for other, left in enumerate(lefts):
            at = 4 * chunk + 2 * other
            value = value + three(left, (factors[at][...], factors[at + 1][...]))
        for at in range(cols):
            held[at, :, start : start + part] = value[:, at * part : (at + 1) * part]
    for shift, out in enumerate(outs):
        out[...] = held[lax.rem(info[3] + shift, cols)]


def cross_call(info, image, factors, cols):
    pieces, rows, piece = image.shape
    length = pieces * piece
    panel = sum(factor[0].shape[1] for factor in factors)
    flat = [value for factor in factors for value in factor]
    share = panel // cols
    vmem = pl.BlockSpec(memory_space=pltpu.VMEM)
    return pl.pallas_call(
        functools.partial(cross_kernel, cols),
        out_shape=[jax.ShapeDtypeStruct((rows, share), jnp.float32)] * cols,
        grid_spec=pltpu.PrefetchScalarGridSpec(
            num_scalar_prefetch=1,
            grid=(),
            in_specs=[vmem] * (1 + len(flat)),
            out_specs=[vmem] * cols,
            scratch_shapes=[
                pltpu.VMEM((4, rows, length // 4), jnp.float32),
                pltpu.VMEM((cols, rows, share), jnp.float32),
            ],
        ),
        compiler_params=pltpu.CompilerParams(vmem_limit_bytes=VMEM),
        cost_estimate=pl.CostEstimate(
            flops=6 * rows * length * panel, bytes_accessed=4 * panel * length, transcendentals=0
        ),
    )(info, image, *flat)


def solution(mesh):
    rows, cols = mesh.shape["row"], mesh.shape["col"]
    assert rows == 2 * cols
    bits = []
    while 2 ** (len(bits) + 1) < rows:
        bits.append(2 ** (len(bits) + 1))
    orders = [bits, bits[::-1]]
    pair = partner(rows, 1)
    plane = [[2 * at + core for at in range(cols)] for core in range(2)]

    def local(top_inverse, coupling, child_inverse, tile_mask):
        row = lax.axis_index("row")
        col = lax.axis_index("col")
        child = row % 2
        panel = child_inverse.shape[2]
        share = panel // cols
        uppers = [[(row // order[at]) % 2 for order in orders] for at in range(2)]
        info = jnp.stack([child] + uppers[0] + [col] + uppers[1]).astype(jnp.int32)

        def pick(value, at):
            return lax.dynamic_index_in_dim(value, at, 0, keepdims=False)

        def ordered(kept, got, axis):
            return jnp.where(
                child == 0,
                jnp.concatenate([kept, got], axis=axis),
                jnp.concatenate([got, kept], axis=axis),
            )

        def send(values, at):
            return [
                lax.ppermute(value, "row", partner(rows, order[at]))
                for value, order in zip(values, orders)
            ]

        def halves(kept, got, at):
            keep = []
            send = []
            for one, two, order in zip(kept, got, orders):
                half = one.shape[0] // 2
                upper = (row // order[at]) % 2
                for start, into in ((upper, keep), (1 - upper, send)):
                    if isinstance(two, tuple):
                        got_part = jnp.where(start == 0, two[0], two[1])
                    else:
                        got_part = lax.dynamic_slice_in_dim(two, start * half, half, 0)
                    into.append(lax.dynamic_slice_in_dim(one, start * half, half, 0) + got_part)
            return keep, send

        def joined(mine, got, at):
            return [
                jnp.where(
                    (row // order[at]) % 2 == 0,
                    jnp.concatenate([one, two], axis=0),
                    jnp.concatenate([two, one], axis=0),
                )
                for one, two, order in zip(mine, got, orders)
            ]

        def cross_sum(total, *sent):
            for shift, block in enumerate(sent, 1):
                total = total + lax.ppermute(
                    block, "col", [(at, (at + shift) % cols) for at in range(cols)]
                )
            return total

        def gram_sum(event):
            gram = 0
            for value in after([pick(child_inverse, child), chil_got], event):
                gram = gram + jnp.einsum(
                    "jv,jw->vw",
                    value,
                    lax.dynamic_slice_in_dim(value, col * share, share, 1),
                    precision=lax.Precision.HIGH,
                    preferred_element_type=jnp.float32,
                )
            for bit in bits[::-1]:
                half = gram.shape[0] // 2
                upper = (row // bit) % 2
                sent = lax.dynamic_slice_in_dim(gram, (1 - upper) * half, half, 0)
                gram = lax.dynamic_slice_in_dim(gram, upper * half, half, 0)
                gram = gram + lax.ppermute(sent, "row", partner(rows, bit))
            return gram

        chil_sent, coup_sent = pick(child_inverse, 1 - child), pick(coupling, 1 - child)
        chil_got = lax.ppermute(chil_sent, "row", pair)
        coup_got = lax.ppermute(coup_sent, "row", pair)
        top_got = lax.ppermute(after(top_inverse, (chil_got, coup_got)), "row", pair)

        def swapped(value, event):
            value = lax.all_to_all(value, "row", 0, 0, axis_index_groups=plane, tiled=True)
            value = lax.all_to_all(value, "col", 0, 0, tiled=True)
            if event:
                value = after(value, event)
            return value, lax.all_to_all(value, "row", 0, 0, axis_index_groups=plane, tiled=True)

        chosen = spans(share)
        count = len(chosen)
        given = (tile_mask, coupling, coup_got, child_inverse, chil_got)
        partials = factor_call(info, *given, chosen[:1], cols)
        partials = partials + factor_call(after(info, partials), *given, chosen[1:], cols)
        factors = []
        sums = []
        gram = None
        for step in range(count + 1):
            if step < count:
                sent_one, kept_one, sent_two, kept_two = partials[step]
                kept, sent = [kept_one, kept_two], [sent_one, sent_two]
                if step == 0:
                    got = after(send(sent, 0), partials[1])
                else:
                    cuts = [jnp.split(value, 2, axis=0) for value in sent]
                    cuts = after(cuts, begun)
                    first_got = send([cut[0] for cut in cuts], 0)
                    got = list(zip(first_got, send([cut[1] for cut in cuts], 0)))
            if step:
                if step < count:
                    image = after(image, first_got)
                summed = image.reshape(-1, image.shape[2])
                summed = lax.psum_scatter(summed, "col", scatter_dimension=0, tiled=True)
                sums.append(summed)
            if step == count:
                break
            for at in range(1, len(bits)):
                kept, sent = halves(kept, got, at)
                got = send(sent, at)
            pieces = [one + two for one, two in zip(kept, got)]
            if step:
                pieces = after(pieces, image)
            if step >= 2:
                pieces = after(pieces, sums[step - 2])
            for at in reversed(range(2, len(bits))):
                pieces = joined(pieces, send(pieces, at), at)
            other = send(pieces, 1)
            got = [send(pieces, 0), send(other, 0)]
            pieces = [pieces[0], other[0], pieces[1], other[1]]
            got = [got[0][0], got[1][0], got[0][1], got[1][1]]
            image, *first = image_call(info, pieces, [top_inverse, top_got], cols, False, [])
            got = after(got, image)
            begun = got
            image, *second = image_call(info, got, [top_inverse, top_got], cols, True, [image])
            factors.append(first + second)
        crosses = []
        outer = []
        for summed in sums:
            summed = after(summed, image)
            if crosses:
                summed = after(summed, values)
            values, ends = turn_call(info, summed, cols)
            outer.append([ends[0], lax.ppermute(ends[1], "row", pair)])
            halfway, values = swapped(values, crosses)
            if gram is None:
                gram = gram_sum(halfway)
            if len(outer) == count:
                kept = jnp.concatenate([ends[0] for ends in outer], axis=0)
                got = jnp.concatenate([ends[1] for ends in outer], axis=0)
                cross_block = ordered(kept[:, None], got[:, None], 1)
                values, cross_block = lax.optimization_barrier((values, cross_block))
            crosses.append(cross_call(info, values, factors, cols))
        block = jnp.concatenate([cross_sum(*cross) for cross in crosses], axis=0) + gram


        half = block.shape[0] // 2
        kept = lax.dynamic_slice_in_dim(block, child * half, half, 0)
        sent = lax.dynamic_slice_in_dim(block, (1 - child) * half, half, 0)
        got = lax.ppermute(sent, "row", pair)
        child_block = ordered(kept[:, None], got[:, None], 1)
        return cross_block, child_block

    in_specs = (P("row", "col"), P(None, "col", "row"), P(None, "row", None), P(None, "col"))
    out_specs = (P("col", None, "row"), P("row", None, "col"))
    return jax.shard_map(local, mesh=mesh, in_specs=in_specs, out_specs=out_specs, check_vma=False)
```
